32 devices in a mesh: groups: 2 (over y), span: 2 (over x), tok: 4 (over z), head: 2 (over core).
Axes of the slice: x: 2, y: 2, z: 4, core: 2. Of those that a mesh axis runs over, the one named last changes fastest.
Arguments:
- queries: bfloat16 [16384, 2, 256], P(('groups', 'span', 'tok'), 'head'), parts along dimension 0, may hold values from -6 to 6
- keys: bfloat16 [16384, 2, 256], P(('groups', 'span', 'tok'), 'head'), parts along dimension 0, may hold values from -6 to 6
- values: bfloat16 [16384, 2, 256], P(('groups', 'span', 'tok'), 'head'), parts along dimension 0, may hold values from -6 to 6
- rates: float32 [16384, 2], P(('groups', 'span', 'tok'), 'head'), parts along dimension 0, may hold values from 0.0001 to 0.001
- w_in: bfloat16 [2, 2, 256, 256], P('head'), may hold values from -0.375 to 0.375
- w_out: bfloat16 [2, 256, 256], P('head'), may hold values from -0.375 to 0.375
- gain: float32 [2, 256], P('head'), may hold values from 0.1 to 1.9
- block_doc: int32 [128], P('groups'), parts along dimension 0, may hold values from 0 to 15, never falling along the last dimension, each value on 1 to 8 neighbouring positions
Outputs:
- mixed: bfloat16 [16384, 2, 256], P(('groups', 'span', 'tok'), 'head'), parts along dimension 0
The draws below stay inside these ranges and needn't reach their ends.
There are 2 independent parts, one for each index of `groups`. The reference program is written for one: setup_inputs(seed, part) draws one part's arguments, and reference() takes and returns one part's arrays. A program takes and returns all parts, laid end to end along the dimension named above; an argument that names none is the same for every part. Nothing has to cross between parts.
Inputs may be any that keep to these rules, and one draw needn't show every extreme that they name: block_doc never falls from one block to the next; each document covers 1 to 8 consecutive blocks, one exactly 8.
All inputs are finite; a program needn't handle non-finite values.
Results may differ from the reference program's by a relative error of at most 0.01.
Values may be sent and summed in bfloat16 or wider, within the bound.
A program may use at most 64 MiB of HBM per device.

```python
import math
import jax
import jax.numpy as jnp
import numpy as np
from jax import lax

DH = 256
FH = 256
HEADS = 2
BLOCK = 128
TOK_DEV = 1024
TOKENS = 8192
BLOCKS = 64
DOCS = 16
N_SPAN = 2
N_TOK = 4


def block_scale(key, extent, cuts, least, largest):
    def one(dim, blocks):
        heights = jax.random.uniform(jax.random.fold_in(jax.random.fold_in(key, 6), dim), (blocks,), jnp.float32, least / len(cuts), largest / len(cuts))
        return jnp.repeat(jnp.exp(heights), extent[dim] // blocks).reshape((-1,) + (1,) * (len(extent) - dim - 1))

    level = one(*cuts[0])
    for cut in cuts[1:]:
        level = level * one(*cut)
    return level


def split_up(count, total, most, slope):
    weights = [(1 << 20) // math.isqrt(standing ** slope) + 1 for standing in range(2, count + 1)]
    spare, given = total - most - (count - 1), [1] * (count - 1)
    while spare > 0:
        candidates = [i for i in range(count - 1) if given[i] < most]
        mass, budget = sum([weights[i] for i in candidates]), spare
        for i in candidates:
            addition = min(most - given[i], max(1, budget * weights[i] // mass), spare)
            given[i] = given[i] + addition
            spare = spare - addition
    return np.array([most] + given)


def uneven_parts(own_key, amount, total, most, lean):
    if amount == 2:
        one = jax.random.randint(own_key, (), max(1, total - most), min(most, total - 1) + 1)
        return jnp.stack([one, total - one])
    sizes = jnp.asarray(split_up(amount, total, most, lean), jnp.int32)
    pairs = (amount - 1) // 2
    donor, receiver = sizes[1:1 + 2 * pairs:2], sizes[2:2 + 2 * pairs:2]
    margin = jnp.minimum(donor - 1, most - receiver)
    passed = jax.random.randint(jax.random.fold_in(own_key, 1), (pairs,), 0, 1 << 20) % (margin + 1)
    sizes = sizes.at[1:1 + 2 * pairs:2].set(donor - passed).at[2:2 + 2 * pairs:2].set(receiver + passed)
    return sizes[jax.random.permutation(jax.random.fold_in(own_key, 2), amount)]


def normal_values(own_key, shape, deviation, most, pieces=(), dtype=jnp.bfloat16):
    loudness = block_scale(own_key, shape, pieces, -0.22, 0.18) if pieces else 1.0
    entries = jax.random.normal(own_key, shape, jnp.float32) * deviation * loudness
    return jnp.minimum(jnp.maximum(entries, -most), most).astype(dtype)


def setup_inputs(seed: int = 0, part: int = 0) -> dict:
    splits = jax.random.split(jax.random.key(seed), 9)
    own_keys = jax.random.split(jax.random.fold_in(splits[8], part), 9)
    return {
        "queries": normal_values(own_keys[0], (TOKENS, HEADS, DH), 1.0, 6.0, ((0, 8), (1, 2))),
        "keys": normal_values(own_keys[1], (TOKENS, HEADS, DH), 1.0, 6.0, ((0, 8), (1, 2))),
        "values": normal_values(own_keys[2], (TOKENS, HEADS, DH), 1.0, 6.0, ((0, 8), (1, 2))),
        "rates": jnp.clip(jnp.exp(math.log(0.001) - 2.3025852 * jax.random.uniform(own_keys[3], (TOKENS, HEADS), jnp.float32) ** block_scale(own_keys[3], (TOKENS, HEADS), ((0, 8), (1, 2)), -0.2, 0.2)), 0.0001, 0.001),
        "w_in": normal_values(splits[4], (HEADS, 2, FH, DH), DH ** -0.5, 0.375, ((0, 2),)),
        "w_out": normal_values(splits[5], (HEADS, DH, FH), FH ** -0.5, 0.375, ((0, 2),)),
        "gain": jnp.clip(1.0 + 0.18 * jax.random.normal(splits[6], (HEADS, DH), jnp.float32), 0.1, 1.9),
        "block_doc": jnp.searchsorted(jnp.cumsum(uneven_parts(own_keys[7], DOCS, BLOCKS, 8, 2)), jnp.arange(BLOCKS), side="right").astype(jnp.int32),
    }


EPSILON = 1e-06
HIGHEST = lax.Precision.HIGHEST

def rms_scale(inputs):
    return inputs * lax.rsqrt(lax.optimization_barrier(jnp.mean(inputs * inputs, axis=-1, keepdims=True)) + EPSILON)

def silu_slope(pre):
    sigmoid_val = jax.nn.sigmoid(pre)
    return sigmoid_val * (1.0 + pre * (1.0 - sigmoid_val))

def renormalize(updated, row_norm):
    scale = row_norm * lax.rsqrt(lax.optimization_barrier(jnp.sum(updated * updated, axis=-1, keepdims=True)) + EPSILON)
    return (updated * scale).astype(jnp.bfloat16)

def rounded_sum(parts):
    narrow = lax.optimization_barrier(parts.astype(jnp.bfloat16))
    return lax.optimization_barrier(jnp.sum(narrow.astype(jnp.float32), axis=0))

def span_gradient(keys_norm, values, rates, w_in, w_out):
    heads = keys_norm.shape[1]
    keys_wide = keys_norm.reshape(N_TOK, TOK_DEV, heads, DH).astype(jnp.float32)
    values_wide = values.reshape(N_TOK, TOK_DEV, heads, DH).astype(jnp.float32)
    rate_rows = rates.reshape(N_TOK, TOK_DEV, heads)
    in_wide = w_in.astype(jnp.float32)
    out_wide = w_out.astype(jnp.float32)
    gate_pre = jnp.einsum('sthd,hfd->sthf', keys_wide, in_wide[:, 0], precision=HIGHEST)
    up_pre = jnp.einsum('sthd,hfd->sthf', keys_wide, in_wide[:, 1], precision=HIGHEST)
    activation = (jax.nn.silu(gate_pre) * up_pre).astype(jnp.bfloat16)
    target = (-(rate_rows[..., None] * values_wide)).astype(jnp.bfloat16)
    act_grad = jnp.einsum('sthd,hdf->sthf', target.astype(jnp.float32), out_wide, precision=HIGHEST)
    gate_grad = (act_grad * up_pre * silu_slope(gate_pre)).astype(jnp.bfloat16)
    up_grad = (act_grad * jax.nn.silu(gate_pre)).astype(jnp.bfloat16)
    stacked = jnp.stack([gate_grad, up_grad], axis=2).astype(jnp.float32)
    grad_in = jnp.einsum('stchf,sthd->shcfd', stacked, keys_wide, precision=HIGHEST)
    grad_out = jnp.einsum('sthd,sthf->shdf', target.astype(jnp.float32), activation.astype(jnp.float32), precision=HIGHEST)
    return (rounded_sum(grad_in), rounded_sum(grad_out))

def apply_fast(query_norm, w_in, w_out):
    query_wide = query_norm.astype(jnp.float32)
    in_wide = w_in.astype(jnp.float32)
    gate_pre = jnp.einsum('thd,hfd->thf', query_wide, in_wide[:, 0], precision=HIGHEST)
    up_pre = jnp.einsum('thd,hfd->thf', query_wide, in_wide[:, 1], precision=HIGHEST)
    activation = (jax.nn.silu(gate_pre) * up_pre).astype(jnp.bfloat16)
    return jnp.einsum('thf,hdf->thd', activation.astype(jnp.float32), w_out.astype(jnp.float32), precision=HIGHEST)

def window_attention(query_norm, keys_norm, values, block_doc):
    tokens, heads, width = query_norm.shape
    block_count = tokens // BLOCK
    shape = (block_count, BLOCK, heads, width)
    zero_block = jnp.zeros((BLOCK, heads, width), jnp.bfloat16)
    prior_keys = jnp.concatenate([zero_block, keys_norm[:-BLOCK]], axis=0)
    prior_values = jnp.concatenate([zero_block, values[:-BLOCK]], axis=0)
    padded_docs = jnp.concatenate([jnp.full((1,), -1, jnp.int32), block_doc.astype(jnp.int32)])
    prior_open = padded_docs[:-1] == padded_docs[1:]
    window_keys = jnp.concatenate([prior_keys.reshape(shape), keys_norm.reshape(shape)], axis=1).astype(jnp.float32)
    window_values = jnp.concatenate([prior_values.reshape(shape), values.reshape(shape)], axis=1).astype(jnp.float32)
    scores = jnp.einsum('nqhd,nkhd->nhqk', query_norm.reshape(shape).astype(jnp.float32), window_keys, precision=HIGHEST) / math.sqrt(width)
    row_pos = lax.broadcasted_iota(jnp.int32, (BLOCK, 2 * BLOCK), 0)
    col_pos = lax.broadcasted_iota(jnp.int32, (BLOCK, 2 * BLOCK), 1)
    inside = col_pos - BLOCK <= row_pos
    visible = jnp.where(col_pos[None] < BLOCK, prior_open[:, None, None], inside[None])
    weights = jnp.where(visible[:, None], jnp.exp(scores), 0.0)
    probabilities = (weights / lax.optimization_barrier(jnp.sum(weights, axis=-1, keepdims=True))).astype(jnp.bfloat16)
    attended = jnp.einsum('nhqk,nkhd->nqhd', probabilities.astype(jnp.float32), window_values, precision=HIGHEST)
    return attended.reshape(tokens, heads, width)

def reference(queries, keys, values, rates, w_in, w_out, gain, block_doc):
    query_norm = rms_scale(queries.astype(jnp.float32)).astype(jnp.bfloat16)
    keys_norm = rms_scale(keys.astype(jnp.float32)).astype(jnp.bfloat16)
    norm_in = jnp.sqrt(lax.optimization_barrier(jnp.sum(jnp.square(w_in.astype(jnp.float32)), axis=-1, keepdims=True)))
    norm_out = jnp.sqrt(lax.optimization_barrier(jnp.sum(jnp.square(w_out.astype(jnp.float32)), axis=-1, keepdims=True)))
    span_len = TOK_DEV * N_TOK
    current_in, current_out = (w_in, w_out)
    outputs = []
    for span_index in range(N_SPAN):
        start = span_index * span_len
        outputs.append(apply_fast(query_norm[start:start + span_len], current_in, current_out))
        if span_index + 1 < N_SPAN:
            grad_in, grad_out = span_gradient(keys_norm[start:start + span_len], values[start:start + span_len], rates[start:start + span_len], current_in, current_out)
            current_in = renormalize(current_in.astype(jnp.float32) - grad_in, norm_in)
            current_out = renormalize(current_out.astype(jnp.float32) - grad_out, norm_out)
    fast_output = jnp.concatenate(outputs, axis=0)
    ttt = rms_scale(fast_output) * gain[None]
    attended = window_attention(query_norm, keys_norm, values, block_doc)
    return (attended + ttt).astype(jnp.bfloat16)
```

```python
import functools

import jax
import jax.numpy as jnp
from jax import lax
from jax.experimental import pallas as pl
from jax.experimental.pallas import tpu as pltpu
from jax.sharding import PartitionSpec as P

BLOCK = 128
TILE = 256
EPSILON = 1e-06
MESH = pl.DeviceIdType.MESH
F32 = jnp.float32
BF16 = jnp.bfloat16


def dot_nt(a, b):
    return lax.dot_general(a, b, (((1,), (1,)), ((), ())), preferred_element_type=F32)


def dot_nn(a, b):
    return lax.dot_general(a, b, (((1,), (0,)), ((), ())), preferred_element_type=F32)


def rms_rows(x):
    return x * lax.rsqrt(jnp.mean(x * x, axis=-1, keepdims=True) + EPSILON)


def sigmoid(x):
    return 0.5 * jnp.tanh(0.5 * x) + 0.5


def kernel(
    spans,
    toks,
    q_ref,
    k_ref,
    v_ref,
    rates_ref,
    w_in_ref,
    w_out_ref,
    gain_ref,
    doc_ref,
    out_ref,
    q_raw,
    k_raw,
    v_ext,
    qn,
    kn,
    rates,
    gain,
    doc,
    cur,
    start_rows,
    gate_t,
    up_t,
    act_t,
    grads,
    parts,
    fresh,
    gate_buf,
    act_buf,
    attended,
    out_buf,
    local_sem,
    out_sem,
    halo_send,
    halo_recv,
    part_send,
    part_recv,
    fresh_send,
    fresh_recv,
):
    tokens, width = q_ref.shape
    hidden = cur.shape[1]
    rows = hidden // toks
    blocks = tokens // BLOCK
    tiles = tokens // TILE
    span = lax.axis_index("span")
    tok = lax.axis_index("tok")
    place = span * toks + tok
    own = pl.ds(pl.multiple_of(tok * rows, rows), rows)

    def at(s, t):
        return {"span": s, "tok": t}

    barrier = pltpu.get_barrier_semaphore()
    for k in range(1, toks):
        pl.semaphore_signal(
            barrier, inc=1, device_id=at(span, lax.rem(tok + k, toks)), device_id_type=MESH
        )

    @pl.when(span < spans - 1)
    def _():
        for k in range(toks):
            pl.semaphore_signal(barrier, inc=1, device_id=at(span + 1, k), device_id_type=MESH)

    @pl.when(span > 0)
    def _():
        for k in range(toks):
            pl.semaphore_signal(barrier, inc=1, device_id=at(span - 1, k), device_id_type=MESH)

    k_load = pltpu.make_async_copy(k_ref, k_raw.at[pl.ds(BLOCK, tokens)], local_sem.at[0])
    v_load = pltpu.make_async_copy(v_ref, v_ext.at[pl.ds(BLOCK, tokens)], local_sem.at[1])
    q_load = pltpu.make_async_copy(q_ref, q_raw, local_sem.at[2])
    rates_load = pltpu.make_async_copy(rates_ref, rates, local_sem.at[3])
    gain_load = pltpu.make_async_copy(gain_ref, gain, local_sem.at[4])
    doc_load = pltpu.make_async_copy(doc_ref, doc, local_sem.at[5])
    in_load = pltpu.make_async_copy(w_in_ref, cur.at[pl.ds(0, 2)], local_sem.at[6])
    w_load = pltpu.make_async_copy(w_out_ref, cur.at[2], local_sem.at[7])
    start_in_load = pltpu.make_async_copy(
        w_in_ref.at[:, own], start_rows.at[pl.ds(0, 2)], local_sem.at[8]
    )
    start_out_load = pltpu.make_async_copy(w_out_ref.at[own], start_rows.at[2], local_sem.at[9])
    k_load.start()

    @pl.when(span == 0)
    def _():
        in_load.start()
        w_load.start()

    v_load.start()
    rates_load.start()
    q_load.start()
    doc_load.start()
    gain_load.start()

    @pl.when(span < spans - 1)
    def _():
        start_in_load.start()
        start_out_load.start()

    sides = 1 if spans == 2 else jnp.minimum(span, 1) + jnp.minimum(spans - 1 - span, 1)
    pl.semaphore_wait(barrier, toks - 1 + toks * sides)

    later = lax.rem(place + 1, spans * toks)
    later_at = at(later // toks, lax.rem(later, toks))
    last_rows = pl.ds(tokens - BLOCK, BLOCK)
    halo_k = pltpu.make_async_remote_copy(
        k_ref.at[last_rows],
        k_raw.at[pl.ds(0, BLOCK)],
        halo_send.at[0],
        halo_recv.at[0],
        device_id=later_at,
        device_id_type=MESH,
    )
    halo_v = pltpu.make_async_remote_copy(
        v_ref.at[last_rows],
        v_ext.at[pl.ds(0, BLOCK)],
        halo_send.at[1],
        halo_recv.at[1],
        device_id=later_at,
        device_id_type=MESH,
    )

    @pl.when(place < spans * toks - 1)
    def _():
        halo_k.start()
        halo_v.start()

    def part_copy(c, k):
        target = lax.rem(tok + k, toks)
        return pltpu.make_async_remote_copy(
            grads.at[c, pl.ds(pl.multiple_of(target * rows, rows), rows)],
            parts.at[c, k - 1],
            part_send.at[c, k - 1],
            part_recv.at[c, k - 1],
            device_id=at(span, target),
            device_id_type=MESH,
        )

    def fresh_copy(c, k):
        return pltpu.make_async_remote_copy(
            fresh.at[c],
            cur.at[c, own],
            fresh_send.at[c, k],
            fresh_recv.at[c, k],
            device_id=at(lax.rem(span + 1, spans), lax.rem(tok + k, toks)),
            device_id_type=MESH,
        )

    def norm_keys():
        k_load.wait()
        for i in range(tiles):
            piece = pl.ds(BLOCK + i * TILE, TILE)
            kn[piece] = rms_rows(k_raw[piece].astype(F32)).astype(BF16)

    def send_gradient():
        w_out_t = cur[2].astype(F32).T.astype(BF16)
        for i in range(tiles):
            piece = pl.ds(BLOCK + i * TILE, TILE)
            lanes = pl.ds(i * TILE, TILE)
            keys = kn[piece]
            gate = dot_nt(cur[0], keys)
            up = dot_nt(cur[1], keys)
            step = -rates[:, lanes]
            act_grad = dot_nt(w_out_t, v_ext[piece]) * step
            s = sigmoid(gate)
            silu = gate * s
            act_t[:, lanes] = (silu * up * step).astype(BF16)
            gate_t[:, lanes] = (act_grad * up * (s + silu * (1.0 - s))).astype(BF16)
            up_t[:, lanes] = (act_grad * silu).astype(BF16)
        keys = kn[pl.ds(BLOCK, tokens)]
        grads[0] = dot_nn(gate_t[...], keys).astype(BF16)
        for k in range(1, toks):
            part_copy(0, k).start()
        grads[1] = dot_nn(up_t[...], keys).astype(BF16)
        for k in range(1, toks):
            part_copy(1, k).start()
        grads[2] = dot_nn(act_t[...], v_ext[pl.ds(BLOCK, tokens)]).T.astype(BF16)
        for k in range(1, toks):
            part_copy(2, k).start()

    def pass_on(c):
        total = grads[c, own].astype(F32)
        for k in range(1, toks):
            part_copy(c, k).wait_recv()
            total += parts[c, k - 1].astype(F32)
        first = start_rows[c].astype(F32)
        updated = cur[c, own].astype(F32) - total
        scale = jnp.sqrt(jnp.sum(first * first, axis=-1, keepdims=True)) * lax.rsqrt(
            jnp.sum(updated * updated, axis=-1, keepdims=True) + EPSILON
        )
        fresh[c] = (updated * scale).astype(BF16)
        for k in range(toks):
            fresh_copy(c, k).start()

    def sent():
        for c in range(3):
            for k in range(1, toks):
                part_copy(c, k).wait_send()
            for k in range(toks):
                fresh_copy(c, k).wait_send()

    def norm_queries():
        q_load.wait()
        for i in range(tiles):
            piece = pl.ds(i * TILE, TILE)
            qn[piece] = rms_rows(q_raw[piece].astype(F32)).astype(BF16)

    def attend():
        doc_load.wait()
        row_pos = lax.broadcasted_iota(jnp.int32, (BLOCK, BLOCK), 0)
        col_pos = lax.broadcasted_iota(jnp.int32, (BLOCK, BLOCK), 1)
        inside = col_pos <= row_pos

        def one(b):
            block = place * blocks + b
            before = doc[jnp.maximum(block - 1, 0)]
            same = jnp.where(before == doc[block], 1.0, 0.0).astype(F32)
            same = jnp.where(block > 0, same, 0.0)
            window = pl.ds(b * BLOCK, 2 * BLOCK)
            score = dot_nt(qn[pl.ds(b * BLOCK, BLOCK)], kn[window]) * (width**-0.5)
            weight = jnp.exp(score)
            prior = weight[:, :BLOCK] * same
            here = jnp.where(inside, weight[:, BLOCK:], 0.0)
            both = jnp.concatenate([prior, here], axis=1)
            total = jnp.sum(both, axis=-1, keepdims=True)
            mixed = dot_nn(both.astype(BF16), v_ext[window])
            attended[pl.ds(b * BLOCK, BLOCK)] = mixed / total

        for b in range(1, blocks):
            one(b)

        @pl.when(place > 0)
        def _():
            halo_k.wait_recv()
            halo_v.wait_recv()

        @pl.when(place == 0)
        def _():
            k_raw[pl.ds(0, BLOCK)] = jnp.zeros((BLOCK, width), BF16)
            v_ext[pl.ds(0, BLOCK)] = jnp.zeros((BLOCK, width), BF16)

        kn[pl.ds(0, BLOCK)] = rms_rows(k_raw[pl.ds(0, BLOCK)].astype(F32)).astype(BF16)
        one(0)

    def out_copy(i):
        piece = pl.ds(i * TILE, TILE)
        return pltpu.make_async_copy(out_buf.at[piece], out_ref.at[piece], out_sem.at[i])

    def apply_fast(ready):
        ready(0)
        for i in range(tiles):
            piece = pl.ds(i * TILE, TILE)
            gate_buf[piece] = dot_nt(qn[piece], cur[0])
        ready(1)
        for i in range(tiles):
            piece = pl.ds(i * TILE, TILE)
            gate = gate_buf[piece]
            up = dot_nt(qn[piece], cur[1])
            act_buf[piece] = (gate * sigmoid(gate) * up).astype(BF16)
        ready(2)
        gain_load.wait()
        for i in range(tiles):
            piece = pl.ds(i * TILE, TILE)
            fast = dot_nt(act_buf[piece], cur[2])
            out_buf[piece] = (attended[piece] + rms_rows(fast) * gain[...]).astype(BF16)
            out_copy(i).start()

    def arrived(c):
        for k in range(toks):
            fresh_copy(c, k).wait_recv()

    @pl.when(span == 0)
    def _():
        norm_keys()
        in_load.wait()
        w_load.wait()
        v_load.wait()
        rates_load.wait()
        start_in_load.wait()
        start_out_load.wait()
        send_gradient()
        norm_queries()
        attend()
        pass_on(0)
        pass_on(1)
        pass_on(2)
        apply_fast(lambda c: None)
        sent()

    @pl.when(span > 0)
    def _():
        norm_keys()
        norm_queries()
        v_load.wait()
        rates_load.wait()
        attend()
        if spans > 2:

            @pl.when(span < spans - 1)
            def _():
                start_in_load.wait()
                start_out_load.wait()
                for c in range(3):
                    arrived(c)
                send_gradient()
                for c in range(3):
                    pass_on(c)
                apply_fast(lambda c: None)
                sent()

            @pl.when(span == spans - 1)
            def _():
                apply_fast(arrived)

        else:
            apply_fast(arrived)

    for i in range(tiles):
        out_copy(i).wait()

    @pl.when(place < spans * toks - 1)
    def _():
        halo_k.wait_send()
        halo_v.wait_send()


def body(spans, toks, queries, keys, values, rates, w_in, w_out, gain, block_doc):
    tokens, _, width = queries.shape
    hidden = w_in.shape[2]
    rows = hidden // toks
    tiles = tokens // TILE
    anywhere = pl.BlockSpec(memory_space=pltpu.HBM)
    dma = pltpu.SemaphoreType.DMA
    out = pl.pallas_call(
        functools.partial(kernel, spans, toks),
        out_shape=jax.ShapeDtypeStruct((tokens, width), BF16),
        in_specs=[anywhere] * 8,
        out_specs=anywhere,
        scratch_shapes=[
            pltpu.VMEM((tokens, width), BF16),
            pltpu.VMEM((tokens + BLOCK, width), BF16),
            pltpu.VMEM((tokens + BLOCK, width), BF16),
            pltpu.VMEM((tokens, width), BF16),
            pltpu.VMEM((tokens + BLOCK, width), BF16),
            pltpu.VMEM((1, tokens), F32),
            pltpu.VMEM((1, width), F32),
            pltpu.SMEM(block_doc.shape, jnp.int32),
            pltpu.VMEM((3, hidden, width), BF16),
            pltpu.VMEM((3, rows, width), BF16),
            pltpu.VMEM((hidden, tokens), BF16),
            pltpu.VMEM((hidden, tokens), BF16),
            pltpu.VMEM((hidden, tokens), BF16),
            pltpu.VMEM((3, hidden, width), BF16),
            pltpu.VMEM((3, toks - 1, rows, width), BF16),
            pltpu.VMEM((3, rows, width), BF16),
            pltpu.VMEM((tokens, hidden), F32),
            pltpu.VMEM((tokens, hidden), BF16),
            pltpu.VMEM((tokens, width), F32),
            pltpu.VMEM((tokens, width), BF16),
            dma((10,)),
            dma((tiles,)),
            dma((2,)),
            dma((2,)),
            dma((3, toks - 1)),
            dma((3, toks - 1)),
            dma((3, toks)),
            dma((3, toks)),
        ],
        compiler_params=pltpu.CompilerParams(
            collective_id=0, has_side_effects=True, vmem_limit_bytes=48 << 20
        ),
    )(
        queries.reshape(tokens, width),
        keys.reshape(tokens, width),
        values.reshape(tokens, width),
        rates.reshape(1, tokens),
        w_in.reshape(w_in.shape[1:]),
        w_out.reshape(w_out.shape[1:]),
        gain,
        block_doc,
    )
    return out.reshape(queries.shape)


def solution(mesh):
    placed = (
        P(("groups", "span", "tok"), "head", None),
        P(("groups", "span", "tok"), "head", None),
        P(("groups", "span", "tok"), "head", None),
        P(("groups", "span", "tok"), "head"),
        P("head", None, None, None),
        P("head", None, None),
        P("head", None),
        P("groups"),
    )
    return jax.shard_map(
        functools.partial(body, mesh.shape["span"], mesh.shape["tok"]),
        mesh=mesh,
        in_specs=placed,
        out_specs=P(("groups", "span", "tok"), "head", None),
        check_vma=False,
    )
```

```python
import functools

import jax
import jax.numpy as jnp
from jax import lax
from jax.experimental import pallas as pl
from jax.experimental.pallas import tpu as pltpu
from jax.sharding import PartitionSpec as P

BLOCK = 128
TILE = 256
EPSILON = 1e-06
MESH = pl.DeviceIdType.MESH
F32 = jnp.float32
BF16 = jnp.bfloat16


def dot_nt(a, b):
    return lax.dot_general(a, b, (((1,), (1,)), ((), ())), preferred_element_type=F32)


def dot_nn(a, b):
    return lax.dot_general(a, b, (((1,), (0,)), ((), ())), preferred_element_type=F32)


def rms_rows(x):
    return x * lax.rsqrt(jnp.mean(x * x, axis=-1, keepdims=True) + EPSILON)


def sigmoid(x):
    return 0.5 * jnp.tanh(0.5 * x) + 0.5


def kernel(
    spans,
    toks,
    q_ref,
    k_ref,
    v_ref,
    rates_ref,
    w_in_ref,
    w_out_ref,
    gain_ref,
    doc_ref,
    out_ref,
    q_raw,
    k_raw,
    v_ext,
    qn,
    kn,
    rates,
    gain,
    doc,
    cur,
    start_rows,
    gate_t,
    up_t,
    act_t,
    grads,
    parts,
    fresh,
    gate_buf,
    act_buf,
    attended,
    out_buf,
    local_sem,
    out_sem,
    halo_send,
    halo_recv,
    part_send,
    part_recv,
    fresh_send,
    fresh_recv,
):
    tokens, width = q_ref.shape
    hidden = cur.shape[1]
    rows = hidden // toks
    blocks = tokens // BLOCK
    tiles = tokens // TILE
    span = lax.axis_index("span")
    tok = lax.axis_index("tok")
    place = span * toks + tok
    own = pl.ds(pl.multiple_of(tok * rows, rows), rows)

    def at(s, t):
        return {"span": s, "tok": t}

    barrier = pltpu.get_barrier_semaphore()
    for k in range(1, toks):
        pl.semaphore_signal(
            barrier, inc=1, device_id=at(span, lax.rem(tok + k, toks)), device_id_type=MESH
        )

    @pl.when(span < spans - 1)
    def _():
        for k in range(toks):
            pl.semaphore_signal(barrier, inc=1, device_id=at(span + 1, k), device_id_type=MESH)

    @pl.when(span > 0)
    def _():
        for k in range(toks):
            pl.semaphore_signal(barrier, inc=1, device_id=at(span - 1, k), device_id_type=MESH)

    k_load = pltpu.make_async_copy(k_ref, k_raw.at[pl.ds(BLOCK, tokens)], local_sem.at[0])
    v_load = pltpu.make_async_copy(v_ref, v_ext.at[pl.ds(BLOCK, tokens)], local_sem.at[1])
    q_load = pltpu.make_async_copy(q_ref, q_raw, local_sem.at[2])
    rates_load = pltpu.make_async_copy(rates_ref, rates, local_sem.at[3])
    gain_load = pltpu.make_async_copy(gain_ref, gain, local_sem.at[4])
    doc_load = pltpu.make_async_copy(doc_ref, doc, local_sem.at[5])
    in_load = pltpu.make_async_copy(w_in_ref, cur.at[pl.ds(0, 2)], local_sem.at[6])
    w_load = pltpu.make_async_copy(w_out_ref, cur.at[2], local_sem.at[7])
    start_in_load = pltpu.make_async_copy(
        w_in_ref.at[:, own], start_rows.at[pl.ds(0, 2)], local_sem.at[8]
    )
    start_out_load = pltpu.make_async_copy(w_out_ref.at[own], start_rows.at[2], local_sem.at[9])
    k_load.start()

    @pl.when(span == 0)
    def _():
        in_load.start()
        w_load.start()

    v_load.start()
    rates_load.start()
    q_load.start()
    doc_load.start()
    gain_load.start()

    @pl.when(span < spans - 1)
    def _():
        start_in_load.start()
        start_out_load.start()

    sides = 1 if spans == 2 else jnp.minimum(span, 1) + jnp.minimum(spans - 1 - span, 1)
    pl.semaphore_wait(barrier, toks - 1 + toks * sides)

    later = lax.rem(place + 1, spans * toks)
    later_at = at(later // toks, lax.rem(later, toks))
    last_rows = pl.ds(tokens - BLOCK, BLOCK)
    halo_k = pltpu.make_async_remote_copy(
        k_ref.at[last_rows],
        k_raw.at[pl.ds(0, BLOCK)],
        halo_send.at[0],
        halo_recv.at[0],
        device_id=later_at,
        device_id_type=MESH,
    )
    halo_v = pltpu.make_async_remote_copy(
        v_ref.at[last_rows],
        v_ext.at[pl.ds(0, BLOCK)],
        halo_send.at[1],
        halo_recv.at[1],
        device_id=later_at,
        device_id_type=MESH,
    )

    @pl.when(place < spans * toks - 1)
    def _():
        halo_k.start()
        halo_v.start()

    def part_copy(c, k):
        target = lax.rem(tok + k, toks)
        return pltpu.make_async_remote_copy(
            grads.at[c, pl.ds(pl.multiple_of(target * rows, rows), rows)],
            parts.at[c, k - 1],
            part_send.at[c, k - 1],
            part_recv.at[c, k - 1],
            device_id=at(span, target),
            device_id_type=MESH,
        )

    def fresh_copy(c, k):
        return pltpu.make_async_remote_copy(
            fresh.at[c],
            cur.at[c, own],
            fresh_send.at[c, k],
            fresh_recv.at[c, k],
            device_id=at(lax.rem(span + 1, spans), lax.rem(tok + k, toks)),
            device_id_type=MESH,
        )

    def norm_keys():
        k_load.wait()
        for i in range(tiles):
            piece = pl.ds(BLOCK + i * TILE, TILE)
            kn[piece] = rms_rows(k_raw[piece].astype(F32)).astype(BF16)

    def send_gradient():
        w_out_t = cur[2].astype(F32).T.astype(BF16)
        for i in range(tiles):
            piece = pl.ds(BLOCK + i * TILE, TILE)
            lanes = pl.ds(i * TILE, TILE)
            keys = kn[piece]
            gate = dot_nt(cur[0], keys)
            up = dot_nt(cur[1], keys)
            step = -rates[:, lanes]
            act_grad = dot_nt(w_out_t, v_ext[piece]) * step
            s = sigmoid(gate)
            silu = gate * s
            act_t[:, lanes] = (silu * up * step).astype(BF16)
            gate_t[:, lanes] = (act_grad * up * (s + silu * (1.0 - s))).astype(BF16)
            up_t[:, lanes] = (act_grad * silu).astype(BF16)
        keys = kn[pl.ds(BLOCK, tokens)]
        grads[0] = dot_nn(gate_t[...], keys).astype(BF16)
        for k in range(1, toks):
            part_copy(0, k).start()
        grads[1] = dot_nn(up_t[...], keys).astype(BF16)
        for k in range(1, toks):
            part_copy(1, k).start()
        grads[2] = dot_nn(act_t[...], v_ext[pl.ds(BLOCK, tokens)]).T.astype(BF16)
        for k in range(1, toks):
            part_copy(2, k).start()

    def pass_on(c):
        total = grads[c, own].astype(F32)
        for k in range(1, toks):
            part_copy(c, k).wait_recv()
            total += parts[c, k - 1].astype(F32)
        first = start_rows[c].astype(F32)
        updated = cur[c, own].astype(F32) - total
        scale = jnp.sqrt(jnp.sum(first * first, axis=-1, keepdims=True)) * lax.rsqrt(
            jnp.sum(updated * updated, axis=-1, keepdims=True) + EPSILON
        )
        fresh[c] = (updated * scale).astype(BF16)
        for k in range(toks):
            fresh_copy(c, k).start()

    def sent():
        for c in range(3):
            for k in range(1, toks):
                part_copy(c, k).wait_send()
            for k in range(toks):
                fresh_copy(c, k).wait_send()

    def norm_queries():
        q_load.wait()
        for i in range(tiles):
            piece = pl.ds(i * TILE, TILE)
            qn[piece] = rms_rows(q_raw[piece].astype(F32)).astype(BF16)

    def attend():
        doc_load.wait()
        row_pos = lax.broadcasted_iota(jnp.int32, (BLOCK, BLOCK), 0)
        col_pos = lax.broadcasted_iota(jnp.int32, (BLOCK, BLOCK), 1)
        inside = col_pos <= row_pos

        def one(b):
            block = place * blocks + b
            before = doc[jnp.maximum(block - 1, 0)]
            same = jnp.where(before == doc[block], 1.0, 0.0).astype(F32)
            same = jnp.where(block > 0, same, 0.0)
            window = pl.ds(b * BLOCK, 2 * BLOCK)
            score = dot_nt(qn[pl.ds(b * BLOCK, BLOCK)], kn[window]) * (width**-0.5)
            weight = jnp.exp(score)
            prior = weight[:, :BLOCK] * same
            here = jnp.where(inside, weight[:, BLOCK:], 0.0)
            both = jnp.concatenate([prior, here], axis=1)
            total = jnp.sum(both, axis=-1, keepdims=True)
            mixed = dot_nn(both.astype(BF16), v_ext[window])
            attended[pl.ds(b * BLOCK, BLOCK)] = mixed / total

        for b in range(1, blocks):
            one(b)

        @pl.when(place > 0)
        def _():
            halo_k.wait_recv()
            halo_v.wait_recv()

        @pl.when(place == 0)
        def _():
            k_raw[pl.ds(0, BLOCK)] = jnp.zeros((BLOCK, width), BF16)
            v_ext[pl.ds(0, BLOCK)] = jnp.zeros((BLOCK, width), BF16)

        kn[pl.ds(0, BLOCK)] = rms_rows(k_raw[pl.ds(0, BLOCK)].astype(F32)).astype(BF16)
        one(0)

    def out_copy(i):
        piece = pl.ds(i * TILE, TILE)
        return pltpu.make_async_copy(out_buf.at[piece], out_ref.at[piece], out_sem.at[i])

    def apply_fast(ready):
        ready(0)
        for i in range(tiles):
            piece = pl.ds(i * TILE, TILE)
            gate_buf[piece] = dot_nt(qn[piece], cur[0])
        ready(1)
        for i in range(tiles):
            piece = pl.ds(i * TILE, TILE)
            gate = gate_buf[piece]
            up = dot_nt(qn[piece], cur[1])
            act_buf[piece] = (gate * sigmoid(gate) * up).astype(BF16)
        ready(2)
        gain_load.wait()
        for i in range(tiles):
            piece = pl.ds(i * TILE, TILE)
            fast = dot_nt(act_buf[piece], cur[2])
            out_buf[piece] = (attended[piece] + rms_rows(fast) * gain[...]).astype(BF16)
            out_copy(i).start()

    def arrived(c):
        for k in range(toks):
            fresh_copy(c, k).wait_recv()

    @pl.when(span == 0)
    def _():
        norm_keys()
        in_load.wait()
        w_load.wait()
        v_load.wait()
        rates_load.wait()
        start_in_load.wait()
        start_out_load.wait()
        send_gradient()
        norm_queries()
        attend()
        pass_on(0)
        pass_on(1)
        pass_on(2)
        apply_fast(lambda c: None)
        sent()

    @pl.when(span > 0)
    def _():
        norm_keys()
        norm_queries()
        v_load.wait()
        rates_load.wait()
        attend()
        if spans > 2:

            @pl.when(span < spans - 1)
            def _():
                start_in_load.wait()
                start_out_load.wait()
                for c in range(3):
                    arrived(c)
                send_gradient()
                for c in range(3):
                    pass_on(c)
                apply_fast(lambda c: None)
                sent()

            @pl.when(span == spans - 1)
            def _():
                apply_fast(arrived)

        else:
            apply_fast(arrived)

    for i in range(tiles):
        out_copy(i).wait()

    @pl.when(place < spans * toks - 1)
    def _():
        halo_k.wait_send()
        halo_v.wait_send()


def body(spans, toks, queries, keys, values, rates, w_in, w_out, gain, block_doc):
    tokens, _, width = queries.shape
    hidden = w_in.shape[2]
    rows = hidden // toks
    tiles = tokens // TILE
    anywhere = pl.BlockSpec(memory_space=pltpu.HBM)
    dma = pltpu.SemaphoreType.DMA
    out = pl.pallas_call(
        functools.partial(kernel, spans, toks),
        out_shape=jax.ShapeDtypeStruct((tokens, width), BF16),
        in_specs=[anywhere] * 8,
        out_specs=anywhere,
        scratch_shapes=[
            pltpu.VMEM((tokens, width), BF16),
            pltpu.VMEM((tokens + BLOCK, width), BF16),
            pltpu.VMEM((tokens + BLOCK, width), BF16),
            pltpu.VMEM((tokens, width), BF16),
            pltpu.VMEM((tokens + BLOCK, width), BF16),
            pltpu.VMEM((1, tokens), F32),
            pltpu.VMEM((1, width), F32),
            pltpu.SMEM(block_doc.shape, jnp.int32),
            pltpu.VMEM((3, hidden, width), BF16),
            pltpu.VMEM((3, rows, width), BF16),
            pltpu.VMEM((hidden, tokens), BF16),
            pltpu.VMEM((hidden, tokens), BF16),
            pltpu.VMEM((hidden, tokens), BF16),
            pltpu.VMEM((3, hidden, width), BF16),
            pltpu.VMEM((3, toks - 1, rows, width), BF16),
            pltpu.VMEM((3, rows, width), BF16),
            pltpu.VMEM((tokens, hidden), F32),
            pltpu.VMEM((tokens, hidden), BF16),
            pltpu.VMEM((tokens, width), F32),
            pltpu.VMEM((tokens, width), BF16),
            dma((10,)),
            dma((tiles,)),
            dma((2,)),
            dma((2,)),
            dma((3, toks - 1)),
            dma((3, toks - 1)),
            dma((3, toks)),
            dma((3, toks)),
        ],
        compiler_params=pltpu.CompilerParams(
            collective_id=0, has_side_effects=True, vmem_limit_bytes=60 << 20
        ),
    )(
        queries.reshape(tokens, width),
        keys.reshape(tokens, width),
        values.reshape(tokens, width),
        rates.reshape(1, tokens),
        w_in.reshape(w_in.shape[1:]),
        w_out.reshape(w_out.shape[1:]),
        gain,
        block_doc,
    )
    return out.reshape(queries.shape)


def solution(mesh):
    placed = (
        P(("groups", "span", "tok"), "head", None),
        P(("groups", "span", "tok"), "head", None),
        P(("groups", "span", "tok"), "head", None),
        P(("groups", "span", "tok"), "head"),
        P("head", None, None, None),
        P("head", None, None),
        P("head", None),
        P("groups"),
    )
    return jax.shard_map(
        functools.partial(body, mesh.shape["span"], mesh.shape["tok"]),
        mesh=mesh,
        in_specs=placed,
        out_specs=P(("groups", "span", "tok"), "head", None),
        check_vma=False,
    )
```

```python
import functools

import jax
import jax.numpy as jnp
from jax import lax
from jax.experimental import pallas as pl
from jax.experimental.pallas import tpu as pltpu
from jax.sharding import PartitionSpec as P

BLOCK = 128
TILE = 256
EPSILON = 1e-06
MESH = pl.DeviceIdType.MESH
F32 = jnp.float32
BF16 = jnp.bfloat16


def dot_nt(a, b):
    return lax.dot_general(a, b, (((1,), (1,)), ((), ())), preferred_element_type=F32)


def dot_nn(a, b):
    return lax.dot_general(a, b, (((1,), (0,)), ((), ())), preferred_element_type=F32)


def rms_rows(x):
    return x * lax.rsqrt(jnp.mean(x * x, axis=-1, keepdims=True) + EPSILON)


def sigmoid(x):
    return 0.5 * jnp.tanh(0.5 * x) + 0.5


def kernel(
    spans,
    toks,
    q_ref,
    k_ref,
    v_ref,
    rates_ref,
    w_in_ref,
    w_out_ref,
    gain_ref,
    doc_ref,
    out_ref,
    q_raw,
    k_raw,
    v_ext,
    qn,
    kn,
    rates,
    gain,
    doc,
    cur,
    start_rows,
    gate_t,
    up_t,
    act_t,
    grads,
    parts,
    fresh,
    gate_buf,
    act_buf,
    attended,
    out_buf,
    local_sem,
    out_sem,
    halo_send,
    halo_recv,
    part_send,
    part_recv,
    fresh_send,
    fresh_recv,
    spread_send,
    spread_recv,
):
    tokens, width = q_ref.shape
    hidden = cur.shape[1]
    rows = hidden // toks
    blocks = tokens // BLOCK
    tiles = tokens // TILE
    span = lax.axis_index("span")
    tok = lax.axis_index("tok")
    place = span * toks + tok
    own = pl.ds(pl.multiple_of(tok * rows, rows), rows)

    def at(s, t):
        return {"span": s, "tok": t}

    barrier = pltpu.get_barrier_semaphore()
    for k in range(1, toks):
        pl.semaphore_signal(
            barrier, inc=1, device_id=at(span, lax.rem(tok + k, toks)), device_id_type=MESH
        )

    @pl.when(span < spans - 1)
    def _():
        for k in range(toks):
            pl.semaphore_signal(barrier, inc=1, device_id=at(span + 1, k), device_id_type=MESH)

    @pl.when(span > 0)
    def _():
        for k in range(toks):
            pl.semaphore_signal(barrier, inc=1, device_id=at(span - 1, k), device_id_type=MESH)

    k_load = pltpu.make_async_copy(k_ref, k_raw.at[pl.ds(BLOCK, tokens)], local_sem.at[0])
    v_load = pltpu.make_async_copy(v_ref, v_ext.at[pl.ds(BLOCK, tokens)], local_sem.at[1])
    q_load = pltpu.make_async_copy(q_ref, q_raw, local_sem.at[2])
    rates_load = pltpu.make_async_copy(rates_ref, rates, local_sem.at[3])
    gain_load = pltpu.make_async_copy(gain_ref, gain, local_sem.at[4])
    doc_load = pltpu.make_async_copy(doc_ref, doc, local_sem.at[5])
    in_load = pltpu.make_async_copy(w_in_ref, cur.at[pl.ds(0, 2)], local_sem.at[6])
    w_load = pltpu.make_async_copy(w_out_ref, cur.at[2], local_sem.at[7])
    start_in_load = pltpu.make_async_copy(
        w_in_ref.at[:, own], start_rows.at[pl.ds(0, 2)], local_sem.at[8]
    )
    start_out_load = pltpu.make_async_copy(w_out_ref.at[own], start_rows.at[2], local_sem.at[9])
    k_load.start()

    @pl.when(span == 0)
    def _():
        in_load.start()
        w_load.start()

    v_load.start()
    rates_load.start()
    q_load.start()
    doc_load.start()
    gain_load.start()

    @pl.when(span < spans - 1)
    def _():
        start_in_load.start()
        start_out_load.start()

    sides = 1 if spans == 2 else jnp.minimum(span, 1) + jnp.minimum(spans - 1 - span, 1)
    pl.semaphore_wait(barrier, toks - 1 + toks * sides)

    later = lax.rem(place + 1, spans * toks)
    later_at = at(later // toks, lax.rem(later, toks))
    last_rows = pl.ds(tokens - BLOCK, BLOCK)
    halo_k = pltpu.make_async_remote_copy(
        k_ref.at[last_rows],
        k_raw.at[pl.ds(0, BLOCK)],
        halo_send.at[0],
        halo_recv.at[0],
        device_id=later_at,
        device_id_type=MESH,
    )
    halo_v = pltpu.make_async_remote_copy(
        v_ref.at[last_rows],
        v_ext.at[pl.ds(0, BLOCK)],
        halo_send.at[1],
        halo_recv.at[1],
        device_id=later_at,
        device_id_type=MESH,
    )

    @pl.when(place < spans * toks - 1)
    def _():
        halo_k.start()
        halo_v.start()

    def part_copy(c, k):
        target = lax.rem(tok + k, toks)
        return pltpu.make_async_remote_copy(
            grads.at[c, pl.ds(pl.multiple_of(target * rows, rows), rows)],
            parts.at[c, k - 1],
            part_send.at[c, k - 1],
            part_recv.at[c, k - 1],
            device_id=at(span, target),
            device_id_type=MESH,
        )

    def fresh_copy(c):
        return pltpu.make_async_remote_copy(
            fresh.at[c],
            cur.at[c, own],
            fresh_send.at[c],
            fresh_recv.at[c],
            device_id=at(lax.rem(span + 1, spans), tok),
            device_id_type=MESH,
        )

    def spread_copy(c, k):
        return pltpu.make_async_remote_copy(
            cur.at[c, own],
            cur.at[c, own],
            spread_send.at[c, k - 1],
            spread_recv.at[c, k - 1],
            device_id=at(span, lax.rem(tok + k, toks)),
            device_id_type=MESH,
        )

    def norm_keys():
        k_load.wait()
        for i in range(tiles):
            piece = pl.ds(BLOCK + i * TILE, TILE)
            kn[piece] = rms_rows(k_raw[piece].astype(F32)).astype(BF16)

    def send_gradient():
        w_out_t = cur[2].astype(F32).T.astype(BF16)
        for i in range(tiles):
            piece = pl.ds(BLOCK + i * TILE, TILE)
            lanes = pl.ds(i * TILE, TILE)
            keys = kn[piece]
            gate = dot_nt(cur[0], keys)
            up = dot_nt(cur[1], keys)
            step = -rates[:, lanes]
            act_grad = dot_nt(w_out_t, v_ext[piece]) * step
            s = sigmoid(gate)
            silu = gate * s
            act_t[:, lanes] = (silu * up * step).astype(BF16)
            gate_t[:, lanes] = (act_grad * up * (s + silu * (1.0 - s))).astype(BF16)
            up_t[:, lanes] = (act_grad * silu).astype(BF16)
        keys = kn[pl.ds(BLOCK, tokens)]
        grads[0] = dot_nn(gate_t[...], keys).astype(BF16)
        for k in range(1, toks):
            part_copy(0, k).start()
        grads[1] = dot_nn(up_t[...], keys).astype(BF16)
        for k in range(1, toks):
            part_copy(1, k).start()
        grads[2] = dot_nn(act_t[...], v_ext[pl.ds(BLOCK, tokens)]).T.astype(BF16)
        for k in range(1, toks):
            part_copy(2, k).start()

    def pass_on(c):
        total = grads[c, own].astype(F32)
        for k in range(1, toks):
            part_copy(c, k).wait_recv()
            total += parts[c, k - 1].astype(F32)
        first = start_rows[c].astype(F32)
        updated = cur[c, own].astype(F32) - total
        scale = jnp.sqrt(jnp.sum(first * first, axis=-1, keepdims=True)) * lax.rsqrt(
            jnp.sum(updated * updated, axis=-1, keepdims=True) + EPSILON
        )
        fresh[c] = (updated * scale).astype(BF16)
        fresh_copy(c).start()

    def sent():
        for c in range(3):
            for k in range(1, toks):
                part_copy(c, k).wait_send()
            fresh_copy(c).wait_send()

    def norm_queries():
        q_load.wait()
        for i in range(tiles):
            piece = pl.ds(i * TILE, TILE)
            qn[piece] = rms_rows(q_raw[piece].astype(F32)).astype(BF16)

    def attend():
        doc_load.wait()
        row_pos = lax.broadcasted_iota(jnp.int32, (BLOCK, BLOCK), 0)
        col_pos = lax.broadcasted_iota(jnp.int32, (BLOCK, BLOCK), 1)
        inside = col_pos <= row_pos

        def one(b):
            block = place * blocks + b
            before = doc[jnp.maximum(block - 1, 0)]
            same = jnp.where(before == doc[block], 1.0, 0.0).astype(F32)
            same = jnp.where(block > 0, same, 0.0)
            window = pl.ds(b * BLOCK, 2 * BLOCK)
            score = dot_nt(qn[pl.ds(b * BLOCK, BLOCK)], kn[window]) * (width**-0.5)
            weight = jnp.exp(score)
            prior = weight[:, :BLOCK] * same
            here = jnp.where(inside, weight[:, BLOCK:], 0.0)
            both = jnp.concatenate([prior, here], axis=1)
            total = jnp.sum(both, axis=-1, keepdims=True)
            mixed = dot_nn(both.astype(BF16), v_ext[window])
            attended[pl.ds(b * BLOCK, BLOCK)] = mixed / total

        for b in range(1, blocks):
            one(b)

        @pl.when(place > 0)
        def _():
            halo_k.wait_recv()
            halo_v.wait_recv()

        @pl.when(place == 0)
        def _():
            k_raw[pl.ds(0, BLOCK)] = jnp.zeros((BLOCK, width), BF16)
            v_ext[pl.ds(0, BLOCK)] = jnp.zeros((BLOCK, width), BF16)

        kn[pl.ds(0, BLOCK)] = rms_rows(k_raw[pl.ds(0, BLOCK)].astype(F32)).astype(BF16)
        one(0)

    def out_copy(i):
        piece = pl.ds(i * TILE, TILE)
        return pltpu.make_async_copy(out_buf.at[piece], out_ref.at[piece], out_sem.at[i])

    def apply_fast(ready):
        ready(0)
        for i in range(tiles):
            piece = pl.ds(i * TILE, TILE)
            gate_buf[piece] = dot_nt(qn[piece], cur[0])
        ready(1)
        for i in range(tiles):
            piece = pl.ds(i * TILE, TILE)
            gate = gate_buf[piece]
            up = dot_nt(qn[piece], cur[1])
            act_buf[piece] = (gate * sigmoid(gate) * up).astype(BF16)
        ready(2)
        gain_load.wait()
        for i in range(tiles):
            piece = pl.ds(i * TILE, TILE)
            fast = dot_nt(act_buf[piece], cur[2])
            out_buf[piece] = (attended[piece] + rms_rows(fast) * gain[...]).astype(BF16)
            out_copy(i).start()

    def arrived(c):
        fresh_copy(c).wait_recv()
        for k in range(1, toks):
            spread_copy(c, k).start()
        for k in range(1, toks):
            spread_copy(c, k).wait_recv()

    @pl.when(span == 0)
    def _():
        norm_keys()
        in_load.wait()
        w_load.wait()
        v_load.wait()
        rates_load.wait()
        start_in_load.wait()
        start_out_load.wait()
        send_gradient()
        norm_queries()
        attend()
        pass_on(0)
        pass_on(1)
        pass_on(2)
        apply_fast(lambda c: None)
        sent()

    @pl.when(span > 0)
    def _():
        norm_keys()
        norm_queries()
        v_load.wait()
        rates_load.wait()
        attend()
        if spans > 2:

            @pl.when(span < spans - 1)
            def _():
                start_in_load.wait()
                start_out_load.wait()
                for c in range(3):
                    arrived(c)
                send_gradient()
                for c in range(3):
                    pass_on(c)
                apply_fast(lambda c: None)
                sent()

            @pl.when(span == spans - 1)
            def _():
                apply_fast(arrived)

        else:
            apply_fast(arrived)
        for c in range(3):
            for k in range(1, toks):
                spread_copy(c, k).wait_send()

    for i in range(tiles):
        out_copy(i).wait()

    @pl.when(place < spans * toks - 1)
    def _():
        halo_k.wait_send()
        halo_v.wait_send()


def body(spans, toks, queries, keys, values, rates, w_in, w_out, gain, block_doc):
    tokens, _, width = queries.shape
    hidden = w_in.shape[2]
    rows = hidden // toks
    tiles = tokens // TILE
    anywhere = pl.BlockSpec(memory_space=pltpu.HBM)
    dma = pltpu.SemaphoreType.DMA
    out = pl.pallas_call(
        functools.partial(kernel, spans, toks),
        out_shape=jax.ShapeDtypeStruct((tokens, width), BF16),
        in_specs=[anywhere] * 8,
        out_specs=anywhere,
        scratch_shapes=[
            pltpu.VMEM((tokens, width), BF16),
            pltpu.VMEM((tokens + BLOCK, width), BF16),
            pltpu.VMEM((tokens + BLOCK, width), BF16),
            pltpu.VMEM((tokens, width), BF16),
            pltpu.VMEM((tokens + BLOCK, width), BF16),
            pltpu.VMEM((1, tokens), F32),
            pltpu.VMEM((1, width), F32),
            pltpu.SMEM(block_doc.shape, jnp.int32),
            pltpu.VMEM((3, hidden, width), BF16),
            pltpu.VMEM((3, rows, width), BF16),
            pltpu.VMEM((hidden, tokens), BF16),
            pltpu.VMEM((hidden, tokens), BF16),
            pltpu.VMEM((hidden, tokens), BF16),
            pltpu.VMEM((3, hidden, width), BF16),
            pltpu.VMEM((3, toks - 1, rows, width), BF16),
            pltpu.VMEM((3, rows, width), BF16),
            pltpu.VMEM((tokens, hidden), F32),
            pltpu.VMEM((tokens, hidden), BF16),
            pltpu.VMEM((tokens, width), F32),
            pltpu.VMEM((tokens, width), BF16),
            dma((10,)),
            dma((tiles,)),
            dma((2,)),
            dma((2,)),
            dma((3, toks - 1)),
            dma((3, toks - 1)),
            dma((3,)),
            dma((3,)),
            dma((3, toks - 1)),
            dma((3, toks - 1)),
        ],
        compiler_params=pltpu.CompilerParams(
            collective_id=0, has_side_effects=True, vmem_limit_bytes=60 << 20
        ),
    )(
        queries.reshape(tokens, width),
        keys.reshape(tokens, width),
        values.reshape(tokens, width),
        rates.reshape(1, tokens),
        w_in.reshape(w_in.shape[1:]),
        w_out.reshape(w_out.shape[1:]),
        gain,
        block_doc,
    )
    return out.reshape(queries.shape)


def solution(mesh):
    placed = (
        P(("groups", "span", "tok"), "head", None),
        P(("groups", "span", "tok"), "head", None),
        P(("groups", "span", "tok"), "head", None),
        P(("groups", "span", "tok"), "head"),
        P("head", None, None, None),
        P("head", None, None),
        P("head", None),
        P("groups"),
    )
    return jax.shard_map(
        functools.partial(body, mesh.shape["span"], mesh.shape["tok"]),
        mesh=mesh,
        in_specs=placed,
        out_specs=P(("groups", "span", "tok"), "head", None),
        check_vma=False,
    )
```

```python
import functools

import jax
import jax.numpy as jnp
from jax import lax
from jax.experimental import pallas as pl
from jax.experimental.pallas import tpu as pltpu
from jax.sharding import PartitionSpec as P

BLOCK = 128
TILE = 256
EPSILON = 1e-06
MESH = pl.DeviceIdType.MESH
F32 = jnp.float32
BF16 = jnp.bfloat16


def dot_nt(a, b):
    return lax.dot_general(a, b, (((1,), (1,)), ((), ())), preferred_element_type=F32)


def dot_nn(a, b):
    return lax.dot_general(a, b, (((1,), (0,)), ((), ())), preferred_element_type=F32)


def rms_rows(x):
    return x * lax.rsqrt(jnp.mean(x * x, axis=-1, keepdims=True) + EPSILON)


def sigmoid(x):
    return 0.5 * jnp.tanh(0.5 * x) + 0.5


def kernel(
    spans,
    toks,
    q_ref,
    k_ref,
    v_ref,
    rates_ref,
    w_in_ref,
    w_out_ref,
    gain_ref,
    doc_ref,
    out_ref,
    q_raw,
    k_raw,
    v_ext,
    qn,
    kn,
    rates,
    gain,
    doc,
    cur,
    start_rows,
    gate_t,
    up_t,
    act_t,
    grads,
    parts,
    fresh,
    gate_buf,
    act_buf,
    attended,
    out_buf,
    local_sem,
    out_sem,
    halo_send,
    halo_recv,
    part_send,
    part_recv,
    fresh_send,
    fresh_recv,
):
    tokens, width = q_ref.shape
    hidden = cur.shape[1]
    rows = hidden // toks
    blocks = tokens // BLOCK
    tiles = tokens // TILE
    span = lax.axis_index("span")
    tok = lax.axis_index("tok")
    place = span * toks + tok
    own = pl.ds(pl.multiple_of(tok * rows, rows), rows)

    def at(s, t):
        return {"span": s, "tok": t}

    barrier = pltpu.get_barrier_semaphore()
    for k in range(1, toks):
        pl.semaphore_signal(
            barrier, inc=1, device_id=at(span, lax.rem(tok + k, toks)), device_id_type=MESH
        )

    @pl.when(span < spans - 1)
    def _():
        for k in range(toks):
            pl.semaphore_signal(barrier, inc=1, device_id=at(span + 1, k), device_id_type=MESH)

    @pl.when(span > 0)
    def _():
        for k in range(toks):
            pl.semaphore_signal(barrier, inc=1, device_id=at(span - 1, k), device_id_type=MESH)

    k_load = pltpu.make_async_copy(k_ref, k_raw.at[pl.ds(BLOCK, tokens)], local_sem.at[0])
    v_load = pltpu.make_async_copy(v_ref, v_ext.at[pl.ds(BLOCK, tokens)], local_sem.at[1])
    q_load = pltpu.make_async_copy(q_ref, q_raw, local_sem.at[2])
    rates_load = pltpu.make_async_copy(rates_ref, rates, local_sem.at[3])
    gain_load = pltpu.make_async_copy(gain_ref, gain, local_sem.at[4])
    doc_load = pltpu.make_async_copy(doc_ref, doc, local_sem.at[5])
    in_load = pltpu.make_async_copy(w_in_ref, cur.at[pl.ds(0, 2)], local_sem.at[6])
    w_load = pltpu.make_async_copy(w_out_ref, cur.at[2], local_sem.at[7])
    start_in_load = pltpu.make_async_copy(
        w_in_ref.at[:, own], start_rows.at[pl.ds(0, 2)], local_sem.at[8]
    )
    start_out_load = pltpu.make_async_copy(w_out_ref.at[own], start_rows.at[2], local_sem.at[9])
    k_load.start()

    @pl.when(span == 0)
    def _():
        in_load.start()
        w_load.start()

    v_load.start()
    rates_load.start()
    q_load.start()
    doc_load.start()
    gain_load.start()

    @pl.when(span < spans - 1)
    def _():
        start_in_load.start()
        start_out_load.start()

    sides = 1 if spans == 2 else jnp.minimum(span, 1) + jnp.minimum(spans - 1 - span, 1)
    pl.semaphore_wait(barrier, toks - 1 + toks * sides)

    later = lax.rem(place + 1, spans * toks)
    later_at = at(later // toks, lax.rem(later, toks))
    last_rows = pl.ds(tokens - BLOCK, BLOCK)
    halo_k = pltpu.make_async_remote_copy(
        k_ref.at[last_rows],
        k_raw.at[pl.ds(0, BLOCK)],
        halo_send.at[0],
        halo_recv.at[0],
        device_id=later_at,
        device_id_type=MESH,
    )
    halo_v = pltpu.make_async_remote_copy(
        v_ref.at[last_rows],
        v_ext.at[pl.ds(0, BLOCK)],
        halo_send.at[1],
        halo_recv.at[1],
        device_id=later_at,
        device_id_type=MESH,
    )

    @pl.when(place < spans * toks - 1)
    def _():
        halo_k.start()
        halo_v.start()

    def part_copy(c, k):
        target = lax.rem(tok + k, toks)
        return pltpu.make_async_remote_copy(
            grads.at[c, pl.ds(pl.multiple_of(target * rows, rows), rows)],
            parts.at[c, k - 1],
            part_send.at[c, k - 1],
            part_recv.at[c, k - 1],
            device_id=at(span, target),
            device_id_type=MESH,
        )

    def fresh_copy(c, k):
        return pltpu.make_async_remote_copy(
            fresh.at[c],
            cur.at[c, own],
            fresh_send.at[c, k],
            fresh_recv.at[c, k],
            device_id=at(lax.rem(span + 1, spans), lax.rem(tok + k, toks)),
            device_id_type=MESH,
        )

    def norm_keys():
        k_load.wait()
        for i in range(tiles):
            piece = pl.ds(BLOCK + i * TILE, TILE)
            kn[piece] = rms_rows(k_raw[piece].astype(F32)).astype(BF16)

    def send_gradient():
        w_out_t = cur[2].astype(F32).T.astype(BF16)
        for i in range(tiles):
            piece = pl.ds(BLOCK + i * TILE, TILE)
            lanes = pl.ds(i * TILE, TILE)
            keys = kn[piece]
            gate = dot_nt(cur[0], keys)
            up = dot_nt(cur[1], keys)
            step = -rates[:, lanes]
            act_grad = dot_nt(w_out_t, v_ext[piece]) * step
            s = sigmoid(gate)
            silu = gate * s
            act_t[:, lanes] = (silu * up * step).astype(BF16)
            gate_t[:, lanes] = (act_grad * up * (s + silu * (1.0 - s))).astype(BF16)
            up_t[:, lanes] = (act_grad * silu).astype(BF16)
        keys = kn[pl.ds(BLOCK, tokens)]
        grads[0] = dot_nn(gate_t[...], keys).astype(BF16)
        for k in range(1, toks):
            part_copy(0, k).start()
        grads[1] = dot_nn(up_t[...], keys).astype(BF16)
        for k in range(1, toks):
            part_copy(1, k).start()
        grads[2] = dot_nn(act_t[...], v_ext[pl.ds(BLOCK, tokens)]).T.astype(BF16)
        for k in range(1, toks):
            part_copy(2, k).start()

    def pass_on(c):
        total = grads[c, own].astype(F32)
        for k in range(1, toks):
            part_copy(c, k).wait_recv()
            total += parts[c, k - 1].astype(F32)
        first = start_rows[c].astype(F32)
        updated = cur[c, own].astype(F32) - total
        scale = jnp.sqrt(jnp.sum(first * first, axis=-1, keepdims=True)) * lax.rsqrt(
            jnp.sum(updated * updated, axis=-1, keepdims=True) + EPSILON
        )
        fresh[c] = (updated * scale).astype(BF16)
        for k in range(toks):
            fresh_copy(c, k).start()

    def sent():
        for c in range(3):
            for k in range(1, toks):
                part_copy(c, k).wait_send()
            for k in range(toks):
                fresh_copy(c, k).wait_send()

    def norm_queries():
        q_load.wait()
        for i in range(tiles):
            piece = pl.ds(i * TILE, TILE)
            qn[piece] = rms_rows(q_raw[piece].astype(F32)).astype(BF16)

    def attend(between=None):
        doc_load.wait()
        row_pos = lax.broadcasted_iota(jnp.int32, (BLOCK, BLOCK), 0)
        col_pos = lax.broadcasted_iota(jnp.int32, (BLOCK, BLOCK), 1)
        inside = col_pos <= row_pos

        def one(b):
            block = place * blocks + b
            before = doc[jnp.maximum(block - 1, 0)]
            same = jnp.where(before == doc[block], 1.0, 0.0).astype(F32)
            same = jnp.where(block > 0, same, 0.0)
            window = pl.ds(b * BLOCK, 2 * BLOCK)
            score = dot_nt(qn[pl.ds(b * BLOCK, BLOCK)], kn[window]) * (width**-0.5)
            weight = jnp.exp(score)
            prior = weight[:, :BLOCK] * same
            here = jnp.where(inside, weight[:, BLOCK:], 0.0)
            both = jnp.concatenate([prior, here], axis=1)
            total = jnp.sum(both, axis=-1, keepdims=True)
            mixed = dot_nn(both.astype(BF16), v_ext[window])
            attended[pl.ds(b * BLOCK, BLOCK)] = mixed / total

        for b in range(1, blocks):
            if between is not None and b in (1, 3, 5):
                between(b // 2)
            one(b)

        @pl.when(place > 0)
        def _():
            halo_k.wait_recv()
            halo_v.wait_recv()

        @pl.when(place == 0)
        def _():
            k_raw[pl.ds(0, BLOCK)] = jnp.zeros((BLOCK, width), BF16)
            v_ext[pl.ds(0, BLOCK)] = jnp.zeros((BLOCK, width), BF16)

        kn[pl.ds(0, BLOCK)] = rms_rows(k_raw[pl.ds(0, BLOCK)].astype(F32)).astype(BF16)
        one(0)

    def out_copy(i):
        piece = pl.ds(i * TILE, TILE)
        return pltpu.make_async_copy(out_buf.at[piece], out_ref.at[piece], out_sem.at[i])

    def apply_fast(ready):
        ready(0)
        for i in range(tiles):
            piece = pl.ds(i * TILE, TILE)
            gate_buf[piece] = dot_nt(qn[piece], cur[0])
        ready(1)
        for i in range(tiles):
            piece = pl.ds(i * TILE, TILE)
            gate = gate_buf[piece]
            up = dot_nt(qn[piece], cur[1])
            act_buf[piece] = (gate * sigmoid(gate) * up).astype(BF16)
        ready(2)
        gain_load.wait()
        for i in range(tiles):
            piece = pl.ds(i * TILE, TILE)
            fast = dot_nt(act_buf[piece], cur[2])
            out_buf[piece] = (attended[piece] + rms_rows(fast) * gain[...]).astype(BF16)
            out_copy(i).start()

    def arrived(c):
        for k in range(toks):
            fresh_copy(c, k).wait_recv()

    @pl.when(span == 0)
    def _():
        norm_keys()
        in_load.wait()
        w_load.wait()
        v_load.wait()
        rates_load.wait()
        start_in_load.wait()
        start_out_load.wait()
        send_gradient()
        norm_queries()
        attend(pass_on)
        apply_fast(lambda c: None)
        sent()

    @pl.when(span > 0)
    def _():
        norm_keys()
        norm_queries()
        v_load.wait()
        rates_load.wait()
        attend()
        if spans > 2:

            @pl.when(span < spans - 1)
            def _():
                start_in_load.wait()
                start_out_load.wait()
                for c in range(3):
                    arrived(c)
                send_gradient()
                for c in range(3):
                    pass_on(c)
                apply_fast(lambda c: None)
                sent()

            @pl.when(span == spans - 1)
            def _():
                apply_fast(arrived)

        else:
            apply_fast(arrived)

    for i in range(tiles):
        out_copy(i).wait()

    @pl.when(place < spans * toks - 1)
    def _():
        halo_k.wait_send()
        halo_v.wait_send()


def body(spans, toks, queries, keys, values, rates, w_in, w_out, gain, block_doc):
    tokens, _, width = queries.shape
    hidden = w_in.shape[2]
    rows = hidden // toks
    tiles = tokens // TILE
    anywhere = pl.BlockSpec(memory_space=pltpu.HBM)
    dma = pltpu.SemaphoreType.DMA
    out = pl.pallas_call(
        functools.partial(kernel, spans, toks),
        out_shape=jax.ShapeDtypeStruct((tokens, width), BF16),
        in_specs=[anywhere] * 8,
        out_specs=anywhere,
        scratch_shapes=[
            pltpu.VMEM((tokens, width), BF16),
            pltpu.VMEM((tokens + BLOCK, width), BF16),
            pltpu.VMEM((tokens + BLOCK, width), BF16),
            pltpu.VMEM((tokens, width), BF16),
            pltpu.VMEM((tokens + BLOCK, width), BF16),
            pltpu.VMEM((1, tokens), F32),
            pltpu.VMEM((1, width), F32),
            pltpu.SMEM(block_doc.shape, jnp.int32),
            pltpu.VMEM((3, hidden, width), BF16),
            pltpu.VMEM((3, rows, width), BF16),
            pltpu.VMEM((hidden, tokens), BF16),
            pltpu.VMEM((hidden, tokens), BF16),
            pltpu.VMEM((hidden, tokens), BF16),
            pltpu.VMEM((3, hidden, width), BF16),
            pltpu.VMEM((3, toks - 1, rows, width), BF16),
            pltpu.VMEM((3, rows, width), BF16),
            pltpu.VMEM((tokens, hidden), F32),
            pltpu.VMEM((tokens, hidden), BF16),
            pltpu.VMEM((tokens, width), F32),
            pltpu.VMEM((tokens, width), BF16),
            dma((10,)),
            dma((tiles,)),
            dma((2,)),
            dma((2,)),
            dma((3, toks - 1)),
            dma((3, toks - 1)),
            dma((3, toks)),
            dma((3, toks)),
        ],
        compiler_params=pltpu.CompilerParams(
            collective_id=0, has_side_effects=True, vmem_limit_bytes=60 << 20
        ),
    )(
        queries.reshape(tokens, width),
        keys.reshape(tokens, width),
        values.reshape(tokens, width),
        rates.reshape(1, tokens),
        w_in.reshape(w_in.shape[1:]),
        w_out.reshape(w_out.shape[1:]),
        gain,
        block_doc,
    )
    return out.reshape(queries.shape)


def solution(mesh):
    placed = (
        P(("groups", "span", "tok"), "head", None),
        P(("groups", "span", "tok"), "head", None),
        P(("groups", "span", "tok"), "head", None),
        P(("groups", "span", "tok"), "head"),
        P("head", None, None, None),
        P("head", None, None),
        P("head", None),
        P("groups"),
    )
    return jax.shard_map(
        functools.partial(body, mesh.shape["span"], mesh.shape["tok"]),
        mesh=mesh,
        in_specs=placed,
        out_specs=P(("groups", "span", "tok"), "head", None),
        check_vma=False,
    )
```

```python
import functools

import jax
import jax.numpy as jnp
from jax import lax
from jax.experimental import pallas as pl
from jax.experimental.pallas import tpu as pltpu
from jax.sharding import PartitionSpec as P

BLOCK = 128
TILE = 256
EPSILON = 1e-06
MESH = pl.DeviceIdType.MESH
F32 = jnp.float32
BF16 = jnp.bfloat16


def dot_nt(a, b):
    return lax.dot_general(a, b, (((1,), (1,)), ((), ())), preferred_element_type=F32)


def dot_nn(a, b):
    return lax.dot_general(a, b, (((1,), (0,)), ((), ())), preferred_element_type=F32)


def rms_rows(x):
    return x * lax.rsqrt(jnp.mean(x * x, axis=-1, keepdims=True) + EPSILON)


def sigmoid(x):
    return 0.5 * jnp.tanh(0.5 * x) + 0.5


def kernel(
    spans,
    toks,
    q_ref,
    k_ref,
    v_ref,
    rates_ref,
    w_in_ref,
    w_out_ref,
    gain_ref,
    doc_ref,
    out_ref,
    q_raw,
    k_raw,
    v_ext,
    qn,
    kn,
    rates,
    gain,
    doc,
    cur,
    start_rows,
    gate_t,
    up_t,
    act_t,
    grads,
    parts,
    fresh,
    gate_buf,
    act_buf,
    attended,
    out_buf,
    local_sem,
    out_sem,
    halo_send,
    halo_recv,
    part_send,
    part_recv,
    fresh_send,
    fresh_recv,
    spread_send,
    spread_recv,
):
    tokens, width = q_ref.shape
    hidden = cur.shape[1]
    rows = hidden // toks
    blocks = tokens // BLOCK
    tiles = tokens // TILE
    span = lax.axis_index("span")
    tok = lax.axis_index("tok")
    place = span * toks + tok
    own = pl.ds(pl.multiple_of(tok * rows, rows), rows)

    def at(s, t):
        return {"span": s, "tok": t}

    barrier = pltpu.get_barrier_semaphore()
    for k in range(1, toks):
        pl.semaphore_signal(
            barrier, inc=1, device_id=at(span, lax.rem(tok + k, toks)), device_id_type=MESH
        )

    @pl.when(span < spans - 1)
    def _():
        for k in range(toks):
            pl.semaphore_signal(barrier, inc=1, device_id=at(span + 1, k), device_id_type=MESH)

    @pl.when(span > 0)
    def _():
        for k in range(toks):
            pl.semaphore_signal(barrier, inc=1, device_id=at(span - 1, k), device_id_type=MESH)

    k_load = pltpu.make_async_copy(k_ref, k_raw.at[pl.ds(BLOCK, tokens)], local_sem.at[0])
    v_load = pltpu.make_async_copy(v_ref, v_ext.at[pl.ds(BLOCK, tokens)], local_sem.at[1])
    q_load = pltpu.make_async_copy(q_ref, q_raw, local_sem.at[2])
    rates_load = pltpu.make_async_copy(rates_ref, rates, local_sem.at[3])
    gain_load = pltpu.make_async_copy(gain_ref, gain, local_sem.at[4])
    doc_load = pltpu.make_async_copy(doc_ref, doc, local_sem.at[5])
    in_load = pltpu.make_async_copy(w_in_ref, cur.at[pl.ds(0, 2)], local_sem.at[6])
    w_load = pltpu.make_async_copy(w_out_ref, cur.at[2], local_sem.at[7])
    start_in_load = pltpu.make_async_copy(
        w_in_ref.at[:, own], start_rows.at[pl.ds(0, 2)], local_sem.at[8]
    )
    start_out_load = pltpu.make_async_copy(w_out_ref.at[own], start_rows.at[2], local_sem.at[9])
    k_load.start()

    @pl.when(span == 0)
    def _():
        in_load.start()
        w_load.start()

    v_load.start()
    rates_load.start()
    q_load.start()
    doc_load.start()
    gain_load.start()

    @pl.when(span < spans - 1)
    def _():
        start_in_load.start()
        start_out_load.start()

    sides = 1 if spans == 2 else jnp.minimum(span, 1) + jnp.minimum(spans - 1 - span, 1)
    pl.semaphore_wait(barrier, toks - 1 + toks * sides)

    later = lax.rem(place + 1, spans * toks)
    later_at = at(later // toks, lax.rem(later, toks))
    last_rows = pl.ds(tokens - BLOCK, BLOCK)
    halo_k = pltpu.make_async_remote_copy(
        k_ref.at[last_rows],
        k_raw.at[pl.ds(0, BLOCK)],
        halo_send.at[0],
        halo_recv.at[0],
        device_id=later_at,
        device_id_type=MESH,
    )
    halo_v = pltpu.make_async_remote_copy(
        v_ref.at[last_rows],
        v_ext.at[pl.ds(0, BLOCK)],
        halo_send.at[1],
        halo_recv.at[1],
        device_id=later_at,
        device_id_type=MESH,
    )

    @pl.when(place < spans * toks - 1)
    def _():
        halo_k.start()
        halo_v.start()

    def part_copy(c, k):
        target = lax.rem(tok + k, toks)
        return pltpu.make_async_remote_copy(
            grads.at[c, pl.ds(pl.multiple_of(target * rows, rows), rows)],
            parts.at[c, k - 1],
            part_send.at[c, k - 1],
            part_recv.at[c, k - 1],
            device_id=at(span, target),
            device_id_type=MESH,
        )

    def fresh_copy(c):
        return pltpu.make_async_remote_copy(
            fresh.at[c],
            cur.at[c, own],
            fresh_send.at[c],
            fresh_recv.at[c],
            device_id=at(lax.rem(span + 1, spans), tok),
            device_id_type=MESH,
        )

    def spread_copy(c, k):
        return pltpu.make_async_remote_copy(
            cur.at[c, own],
            cur.at[c, own],
            spread_send.at[c, k - 1],
            spread_recv.at[c, k - 1],
            device_id=at(span, lax.rem(tok + k, toks)),
            device_id_type=MESH,
        )

    def norm_keys():
        k_load.wait()
        for i in range(tiles):
            piece = pl.ds(BLOCK + i * TILE, TILE)
            kn[piece] = rms_rows(k_raw[piece].astype(F32)).astype(BF16)

    def send_gradient():
        w_out_t = cur[2].astype(F32).T.astype(BF16)
        for i in range(tiles):
            piece = pl.ds(BLOCK + i * TILE, TILE)
            lanes = pl.ds(i * TILE, TILE)
            keys = kn[piece]
            gate = dot_nt(cur[0], keys)
            up = dot_nt(cur[1], keys)
            step = -rates[:, lanes]
            act_grad = dot_nt(w_out_t, v_ext[piece]) * step
            s = sigmoid(gate)
            silu = gate * s
            act_t[:, lanes] = (silu * up * step).astype(BF16)
            gate_t[:, lanes] = (act_grad * up * (s + silu * (1.0 - s))).astype(BF16)
            up_t[:, lanes] = (act_grad * silu).astype(BF16)
        keys = kn[pl.ds(BLOCK, tokens)]
        grads[0] = dot_nn(gate_t[...], keys).astype(BF16)
        for k in range(1, toks):
            part_copy(0, k).start()
        grads[1] = dot_nn(up_t[...], keys).astype(BF16)
        for k in range(1, toks):
            part_copy(1, k).start()
        grads[2] = dot_nn(act_t[...], v_ext[pl.ds(BLOCK, tokens)]).T.astype(BF16)
        for k in range(1, toks):
            part_copy(2, k).start()

    def pass_on(c):
        total = grads[c, own].astype(F32)
        for k in range(1, toks):
            part_copy(c, k).wait_recv()
            total += parts[c, k - 1].astype(F32)
        first = start_rows[c].astype(F32)
        updated = cur[c, own].astype(F32) - total
        scale = jnp.sqrt(jnp.sum(first * first, axis=-1, keepdims=True)) * lax.rsqrt(
            jnp.sum(updated * updated, axis=-1, keepdims=True) + EPSILON
        )
        fresh[c] = (updated * scale).astype(BF16)
        fresh_copy(c).start()

    def sent():
        for c in range(3):
            for k in range(1, toks):
                part_copy(c, k).wait_send()
            fresh_copy(c).wait_send()

    def norm_queries():
        q_load.wait()
        for i in range(tiles):
            piece = pl.ds(i * TILE, TILE)
            qn[piece] = rms_rows(q_raw[piece].astype(F32)).astype(BF16)

    def attend(between=None):
        doc_load.wait()
        row_pos = lax.broadcasted_iota(jnp.int32, (BLOCK, BLOCK), 0)
        col_pos = lax.broadcasted_iota(jnp.int32, (BLOCK, BLOCK), 1)
        inside = col_pos <= row_pos

        def one(b):
            block = place * blocks + b
            before = doc[jnp.maximum(block - 1, 0)]
            same = jnp.where(before == doc[block], 1.0, 0.0).astype(F32)
            same = jnp.where(block > 0, same, 0.0)
            window = pl.ds(b * BLOCK, 2 * BLOCK)
            score = dot_nt(qn[pl.ds(b * BLOCK, BLOCK)], kn[window]) * (width**-0.5)
            weight = jnp.exp(score)
            prior = weight[:, :BLOCK] * same
            here = jnp.where(inside, weight[:, BLOCK:], 0.0)
            both = jnp.concatenate([prior, here], axis=1)
            total = jnp.sum(both, axis=-1, keepdims=True)
            mixed = dot_nn(both.astype(BF16), v_ext[window])
            attended[pl.ds(b * BLOCK, BLOCK)] = mixed / total

        for b in range(1, blocks):
            if between is not None and b in (1, 3, 5):
                between(b // 2)
            one(b)

        @pl.when(place > 0)
        def _():
            halo_k.wait_recv()
            halo_v.wait_recv()

        @pl.when(place == 0)
        def _():
            k_raw[pl.ds(0, BLOCK)] = jnp.zeros((BLOCK, width), BF16)
            v_ext[pl.ds(0, BLOCK)] = jnp.zeros((BLOCK, width), BF16)

        kn[pl.ds(0, BLOCK)] = rms_rows(k_raw[pl.ds(0, BLOCK)].astype(F32)).astype(BF16)
        one(0)

    def out_copy(i):
        piece = pl.ds(i * TILE, TILE)
        return pltpu.make_async_copy(out_buf.at[piece], out_ref.at[piece], out_sem.at[i])

    def apply_fast(ready):
        ready(0)
        for i in range(tiles):
            piece = pl.ds(i * TILE, TILE)
            gate_buf[piece] = dot_nt(qn[piece], cur[0])
        ready(1)
        for i in range(tiles):
            piece = pl.ds(i * TILE, TILE)
            gate = gate_buf[piece]
            up = dot_nt(qn[piece], cur[1])
            act_buf[piece] = (gate * sigmoid(gate) * up).astype(BF16)
        ready(2)
        gain_load.wait()
        for i in range(tiles):
            piece = pl.ds(i * TILE, TILE)
            fast = dot_nt(act_buf[piece], cur[2])
            out_buf[piece] = (attended[piece] + rms_rows(fast) * gain[...]).astype(BF16)
            out_copy(i).start()

    def arrived(c):
        if c == 0:
            for d in range(3):
                fresh_copy(d).wait_recv()
                for k in range(1, toks):
                    spread_copy(d, k).start()
        for k in range(1, toks):
            spread_copy(c, k).wait_recv()

    @pl.when(span == 0)
    def _():
        norm_keys()
        in_load.wait()
        w_load.wait()
        v_load.wait()
        rates_load.wait()
        start_in_load.wait()
        start_out_load.wait()
        send_gradient()
        norm_queries()
        attend(pass_on)
        apply_fast(lambda c: None)
        sent()

    @pl.when(span > 0)
    def _():
        norm_keys()
        norm_queries()
        v_load.wait()
        rates_load.wait()
        attend()
        if spans > 2:

            @pl.when(span < spans - 1)
            def _():
                start_in_load.wait()
                start_out_load.wait()
                for c in range(3):
                    arrived(c)
                send_gradient()
                for c in range(3):
                    pass_on(c)
                apply_fast(lambda c: None)
                sent()

            @pl.when(span == spans - 1)
            def _():
                apply_fast(arrived)

        else:
            apply_fast(arrived)
        for c in range(3):
            for k in range(1, toks):
                spread_copy(c, k).wait_send()

    for i in range(tiles):
        out_copy(i).wait()

    @pl.when(place < spans * toks - 1)
    def _():
        halo_k.wait_send()
        halo_v.wait_send()


def body(spans, toks, queries, keys, values, rates, w_in, w_out, gain, block_doc):
    tokens, _, width = queries.shape
    hidden = w_in.shape[2]
    rows = hidden // toks
    tiles = tokens // TILE
    anywhere = pl.BlockSpec(memory_space=pltpu.HBM)
    dma = pltpu.SemaphoreType.DMA
    out = pl.pallas_call(
        functools.partial(kernel, spans, toks),
        out_shape=jax.ShapeDtypeStruct((tokens, width), BF16),
        in_specs=[anywhere] * 8,
        out_specs=anywhere,
        scratch_shapes=[
            pltpu.VMEM((tokens, width), BF16),
            pltpu.VMEM((tokens + BLOCK, width), BF16),
            pltpu.VMEM((tokens + BLOCK, width), BF16),
            pltpu.VMEM((tokens, width), BF16),
            pltpu.VMEM((tokens + BLOCK, width), BF16),
            pltpu.VMEM((1, tokens), F32),
            pltpu.VMEM((1, width), F32),
            pltpu.SMEM(block_doc.shape, jnp.int32),
            pltpu.VMEM((3, hidden, width), BF16),
            pltpu.VMEM((3, rows, width), BF16),
            pltpu.VMEM((hidden, tokens), BF16),
            pltpu.VMEM((hidden, tokens), BF16),
            pltpu.VMEM((hidden, tokens), BF16),
            pltpu.VMEM((3, hidden, width), BF16),
            pltpu.VMEM((3, toks - 1, rows, width), BF16),
            pltpu.VMEM((3, rows, width), BF16),
            pltpu.VMEM((tokens, hidden), F32),
            pltpu.VMEM((tokens, hidden), BF16),
            pltpu.VMEM((tokens, width), F32),
            pltpu.VMEM((tokens, width), BF16),
            dma((10,)),
            dma((tiles,)),
            dma((2,)),
            dma((2,)),
            dma((3, toks - 1)),
            dma((3, toks - 1)),
            dma((3,)),
            dma((3,)),
            dma((3, toks - 1)),
            dma((3, toks - 1)),
        ],
        compiler_params=pltpu.CompilerParams(
            collective_id=0, has_side_effects=True, vmem_limit_bytes=60 << 20
        ),
    )(
        queries.reshape(tokens, width),
        keys.reshape(tokens, width),
        values.reshape(tokens, width),
        rates.reshape(1, tokens),
        w_in.reshape(w_in.shape[1:]),
        w_out.reshape(w_out.shape[1:]),
        gain,
        block_doc,
    )
    return out.reshape(queries.shape)


def solution(mesh):
    placed = (
        P(("groups", "span", "tok"), "head", None),
        P(("groups", "span", "tok"), "head", None),
        P(("groups", "span", "tok"), "head", None),
        P(("groups", "span", "tok"), "head"),
        P("head", None, None, None),
        P("head", None, None),
        P("head", None),
        P("groups"),
    )
    return jax.shard_map(
        functools.partial(body, mesh.shape["span"], mesh.shape["tok"]),
        mesh=mesh,
        in_specs=placed,
        out_specs=P(("groups", "span", "tok"), "head", None),
        check_vma=False,
    )
```
